128 devices in a mesh: depth: 2 (over core), row: 4 (over x), col: 16 (over z, y).
Axes of the slice: x: 4, y: 4, z: 4, core: 2. Of those that a mesh axis runs over, the one named last changes fastest.
Arguments:
- tokens: bfloat16 [512, 6144], P(('depth', 'col'), 'row'), may hold values from -6 to 6
- up_weight: bfloat16 [6144, 24576], P('row', ('col', 'depth')), may hold values from -0.109375 to 0.109375
- down_weight: bfloat16 [24576, 6144], P(('col', 'depth'), 'row'), may hold values from -0.0546875 to 0.0546875
- grad_out: bfloat16 [512, 6144], P(('depth', 'col'), 'row'), may hold values from -6 to 6
- block_mask: int32 [2, 96, 24], replicated, may hold values 0 or 1
Outputs:
- out: bfloat16 [512, 6144], P(('depth', 'col'), 'row')
- grad_tokens: bfloat16 [512, 6144], P(('depth', 'col'), 'row')
- grad_up: bfloat16 [6144, 24576], P('row', ('col', 'depth'))
- grad_down: bfloat16 [24576, 6144], P(('col', 'depth'), 'row')
The draws below stay inside these ranges and needn't reach their ends.
All inputs are finite; a program needn't handle non-finite values.
Results may differ from the reference program's by a relative error of at most 0.03.
Values may be sent and summed in bfloat16 or wider, within the bound.
A program may use at most 128 MiB of HBM per device.

```python
import jax
import jax.numpy as jnp
from jax import lax

D = 6144
FF = 24576
BLOCK = 256
TOKENS = 512
FFB = 96
DB = 24
N_DEPTH = 2
N_ROW = 4
N_COL = 16


def touch_ends(values, own_key, smallest, top_value):
    index_at = [jax.random.randint(jax.random.fold_in(own_key, axis), (), 0, length) for axis, length in enumerate(values.shape)]
    widest = values.shape.index(max(values.shape))
    beside = index_at[:widest] + [(index_at[widest] + 1) % values.shape[widest]] + index_at[widest + 1:]
    return values.at[tuple(index_at)].set(smallest).at[tuple(beside)].set(top_value)


def shard_levels(key, dims, shards, least, top_value):
    def one(dim, shards_of):
        steps = jax.random.uniform(jax.random.fold_in(jax.random.fold_in(key, 6), dim), (shards_of,), jnp.float32, least / len(shards), top_value / len(shards))
        return jnp.repeat(jnp.exp(steps), dims[dim] // shards_of).reshape((-1,) + (1,) * (len(dims) - dim - 1))

    loudness = one(*shards[0])
    for cut in shards[1:]:
        loudness = loudness * one(*cut)
    return loudness


def bell_draw(own_key, extent, deviation, reach, shards=(), dtype=jnp.bfloat16):
    array = jax.random.normal(own_key, extent, jnp.float32) * deviation
    if len(shards) > 0:
        array = shard_levels(own_key, extent, shards, -0.22, 0.18) * array
    return jnp.clip(array, min=-reach, max=reach).astype(dtype)


def setup_inputs(seed: int = 0) -> dict:
    seeds = jax.random.split(jax.random.key(seed), 6)
    tokens = bell_draw(seeds[0], (TOKENS, D), 1.0, 6.0, ((0, 32), (1, 4)))
    up_weight = bell_draw(seeds[1], (D, FF), (D // 2) ** -0.5, 0.109375, ((0, 4), (1, 32)))
    down_weight = bell_draw(seeds[2], (FF, D), (FF // 2) ** -0.5, 0.0546875, ((0, 32), (1, 4)))
    grad_out = bell_draw(seeds[3], (TOKENS, D), 1.0, 6.0, ((0, 32), (1, 4)))
    block_mask = touch_ends((jax.random.randint(seeds[4], (2, FFB, DB), 0, 2) < 1).astype(jnp.int32), jax.random.fold_in(seeds[4], 1), 0, 1)
    return dict(tokens=tokens, up_weight=up_weight, down_weight=down_weight, grad_out=grad_out, block_mask=block_mask)


gelu_scale = 0.7978845608028654
gelu_cubic = 0.044715


def gelu_value(pre):
    inner = gelu_scale * (pre + gelu_cubic * pre * pre * pre)
    return 0.5 * pre * (1.0 + jnp.tanh(inner))


def gelu_slope(pre):
    inner = gelu_scale * (pre + gelu_cubic * pre * pre * pre)
    bend = jnp.tanh(inner)
    return 0.5 * (1.0 + bend) + 0.5 * pre * (1.0 - bend * bend) * gelu_scale * (1.0 + 3.0 * gelu_cubic * pre * pre)


def expand_mask(mask_part):
    spread = jnp.broadcast_to(mask_part[:, None, :, None], (FFB, BLOCK, DB, BLOCK))
    return spread.reshape(FFB * BLOCK, DB * BLOCK).astype(jnp.bfloat16)


def grouped_product(left, right, groups):
    width = left.shape[1] // groups
    left_parts = jnp.transpose(left.reshape(left.shape[0], groups, width), (1, 0, 2))
    right_parts = right.reshape(groups, width, right.shape[1])

    def step(total, pair):
        part = jnp.dot(pair[0], pair[1], preferred_element_type=jnp.float32)
        return total + part.astype(jnp.bfloat16).astype(jnp.float32), None

    start = jnp.zeros((left.shape[0], right.shape[1]), jnp.float32)
    total, _ = lax.scan(step, start, (left_parts, right_parts))
    return total


def reference(tokens, up_weight, down_weight, grad_out, block_mask):
    up_mask = expand_mask(block_mask[0]).T
    down_mask = expand_mask(block_mask[1])
    up_used = up_weight * up_mask
    down_used = down_weight * down_mask
    pre = grouped_product(tokens, up_used, N_ROW)
    act = gelu_value(pre).astype(jnp.bfloat16)
    out = grouped_product(act, down_used, N_COL * N_DEPTH).astype(jnp.bfloat16)
    grad_act = grouped_product(grad_out, down_used.T, N_ROW)
    grad_pre = (grad_act * gelu_slope(pre)).astype(jnp.bfloat16)
    grad_tokens = grouped_product(grad_pre, up_used.T, N_COL * N_DEPTH).astype(jnp.bfloat16)
    grad_up = (jnp.dot(tokens.T, grad_pre, preferred_element_type=jnp.float32) * up_mask).astype(jnp.bfloat16)
    grad_down = (jnp.dot(act.T, grad_out, preferred_element_type=jnp.float32) * down_mask).astype(jnp.bfloat16)
    return (out, grad_tokens, grad_up, grad_down)
```

```python
import jax
import jax.numpy as jnp
from jax import lax
from jax.experimental import pallas as pl
from jax.experimental.pallas import tpu as pltpu
from jax.sharding import PartitionSpec as P

BLOCK = 256
RING = 4
MESH = pl.DeviceIdType.MESH

gelu_scale = 0.7978845608028654
gelu_cubic = 0.044715

SCHEDULE = (
    [("mm", 0, 0), ("pass", 0), ("pass", 1), ("mm", 0, 3), ("comb", 0, 0), ("mm", 0, 1), ("comb", 0, 3)]
    + [("last", 0), ("last", 1), ("mm", 0, 2), ("comb", 0, 1), ("fin", 0, 0)]
    + [("mm", 1, 2), ("comb", 0, 2), ("fin", 0, 3)]
    + [("mm", 1, 1), ("comb", 1, 2), ("fin", 0, 1), ("fin", 0, 2)]
    + [("mm", 1, 3), ("comb", 1, 1), ("agf", 0, 0)]
    + [("mm", 1, 0), ("comb", 1, 3), ("fin", 1, 2), ("agf", 0, 3), ("agf", 0, 1)]
    + [("comb", 1, 0), ("fin", 1, 1), ("agf", 0, 2), ("om", 0, 0), ("fin", 1, 3), ("om", 0, 3)]
    + [("fin", 1, 0), ("agf", 1, 2), ("agf", 1, 1), ("om", 0, 1), ("zs", 0, 0), ("zs", 0, 3), ("om", 0, 2)]
    + [("agf", 1, 3), ("agf", 1, 0), ("zs", 0, 1), ("zs", 0, 2)]
    + [("om", 1, 2), ("zc", 0), ("om", 1, 1), ("zs", 1, 2), ("zf", 0), ("om", 1, 3), ("zs", 1, 1)]
    + [("om", 1, 0), ("zs", 1, 3), ("zc", 1), ("zs", 1, 0), ("yf", 0), ("tt",), ("at",), ("gdn",)]
    + [("zf", 1), ("gup",), ("yf", 1)]
)


def gelu_pair(pre):
    inner = gelu_scale * (pre + gelu_cubic * pre * pre * pre)
    bend = jnp.tanh(inner)
    value = 0.5 * pre * (1.0 + bend)
    slope = 0.5 * (1.0 + bend) + 0.5 * pre * (1.0 - bend * bend) * gelu_scale * (
        1.0 + 3.0 * gelu_cubic * pre * pre
    )
    return value, slope


def kernel(
    tok_h, up_h, down_h, gout_h, mask_h,
    out_h, gtok_h, gup_h, gdown_h,
    feats, wu, wd, masks, part, own_part, relay, comb_out, comb_in, slopes, hidden,
    pair_out, pair_in, kept, zsend, zrelay, zown, zcomb_out, zcomb_in, fsend, fown, frecv,
    small, tok_t, act_t, gup_v, gdown_v,
    send_sem, recv_sem, local_sem,
):
    f32, bf16 = jnp.float32, jnp.bfloat16
    width = wu.shape[0]
    hid = wu.shape[1]
    x = lax.axis_index("row")
    col = lax.axis_index("col")
    d = lax.axis_index("depth")
    z, y = lax.div(col, RING), lax.rem(col, RING)
    other = 1 - d
    major, minor = (z, y), (y, z)

    def turn(value, by):
        return lax.rem(value + by, RING)

    def major_peer(s, by):
        return {"col": turn(z, by) * RING + y} if s == 0 else {"col": z * RING + turn(y, by)}

    def minor_peer(s, by):
        return major_peer(1 - s, by)

    def row_peer(by):
        return {"row": turn(x, by)}

    sibling = {"depth": other}
    numbers = {}

    def remote(name, src, dst, peer):
        n = numbers.setdefault(name, len(numbers))
        return pltpu.make_async_remote_copy(
            src_ref=src, dst_ref=dst, send_sem=send_sem.at[n], recv_sem=recv_sem.at[n],
            device_id=peer, device_id_type=MESH,
        )

    sent = []

    def send(name, src, dst, peer):
        copy = remote(name, src, dst, peer)
        copy.start()
        sent.append(copy)

    def arrived(name, dst):
        remote(name, dst, dst, sibling).wait_recv()

    sources = (tok_h, gout_h)
    loads = [
        pltpu.make_async_copy(sources[0], feats.at[0, z, y, d], local_sem.at[0]),
        pltpu.make_async_copy(sources[1], feats.at[1, y, z, d], local_sem.at[1]),
        pltpu.make_async_copy(up_h, wu, local_sem.at[2]),
        pltpu.make_async_copy(mask_h, masks, local_sem.at[4]),
        pltpu.make_async_copy(down_h, wd, local_sem.at[3]),
    ]
    for load in loads:
        load.start()

    peers = [row_peer(1), row_peer(3), sibling]
    for by in (1, 2, 3):
        peers += [minor_peer(0, by), minor_peer(1, by)]
    barrier = pltpu.get_barrier_semaphore()
    for peer in peers:
        pl.semaphore_signal(barrier, inc=1, device_id=peer, device_id_type=MESH)
    pl.semaphore_wait(barrier, len(peers))

    hidden_corner = (col * 2 + d) * (hid // BLOCK)
    feature_corner = x * (width // BLOCK)

    def mask_at(which, hb, fb):
        return masks[which, hidden_corner + hb, feature_corner + fb].astype(f32)

    for s in (0, 1):
        for by in (1, 3, 2):
            send(("g1", s, by), sources[s], feats.at[s, major[s], minor[s], d], minor_peer(s, by))
    loads[3].wait()
    loads[2].wait()
    for fb in range(width // BLOCK):
        for hb in range(hid // BLOCK):
            tile = (pl.ds(fb * BLOCK, BLOCK), pl.ds(hb * BLOCK, BLOCK))
            wu[tile] = wu[tile] * mask_at(0, hb, fb).astype(bf16)
    for s in (0, 1):
        loads[s].wait()
        for by in (1, 3, 2):
            arrived(("g1", s, by), feats.at[s, major[s], turn(minor[s], RING - by), d])
        mine = feats.at[s, major[s], :, d]
        send(("g2", s, 1), mine, mine, major_peer(s, 1))
        send(("g2", s, 3), mine, mine, major_peer(s, 3))
        send(("pair", s, 0), mine, mine, sibling)
    loads[4].wait()
    for fb in range(width // BLOCK):
        for hb in range(hid // BLOCK):
            tile = (pl.ds(hb * BLOCK, BLOCK), pl.ds(fb * BLOCK, BLOCK))
            wd[tile] = wd[tile] * mask_at(1, hb, fb).astype(bf16)

    def do_pass(s):
        for by, half in ((1, 0), (3, 2)):
            a = turn(major[s], RING - by)
            whole = feats.at[s, a, :, d]
            arrived(("g2", s, by), whole)
            part_of = feats.at[s, a, pl.ds(half, 2), d]
            send(("g3", s, by), part_of, part_of, major_peer(s, by))
            send(("pair", s, RING - by), whole, whole, sibling)

    def do_last(s):
        a = turn(major[s], 2)
        for by, half in ((1, 0), (3, 2)):
            part_of = feats.at[s, a, pl.ds(half, 2), d]
            arrived(("g3", s, by), part_of)
            send(("pair2", s, by), part_of, part_of, sibling)

    def places(s, k):
        a = turn(major[s], k)
        return a, turn(x + RING - a, 0)

    def product(s, left, tile):
        if s == 0:
            return jnp.dot(left, wu[:, tile], preferred_element_type=f32)
        return lax.dot_general(
            left, wd[tile, :], (((1,), (1,)), ((), ())), preferred_element_type=f32
        )

    def product_back(s, left, tile):
        if s == 0:
            return jnp.dot(left, wd[:, tile], preferred_element_type=f32)
        return lax.dot_general(
            left, wu[tile, :], (((1,), (1,)), ((), ())), preferred_element_type=f32
        )

    def do_mm(s, k):
        a, m = places(s, k)
        if k == 2:
            for by, half in ((1, 0), (3, 2)):
                arrived(("pair2", s, by), feats.at[s, a, pl.ds(half, 2), other])
        else:
            arrived(("pair", s, k), feats.at[s, a, :, other])
        left = jnp.concatenate(
            [feats[s, a, turn(m, j)].reshape(32, width) for j in range(RING)], axis=0
        )
        for n in range(hid // BLOCK):
            tile = pl.ds(n * BLOCK, BLOCK)
            value = product(s, left, tile)
            part[s, k, :, :, tile] = value.astype(bf16).reshape(8, 16, BLOCK)
            own_part[s, k, :, :, tile] = value[:32].reshape(2, 16, BLOCK)
        send(("x1", s, k, 1), part.at[s, k, pl.ds(3, 2)], relay.at[s, 0, k], row_peer(1))
        send(("x1", s, k, 3), part.at[s, k, pl.ds(5, 2)], relay.at[s, 1, k], row_peer(3))

    def do_comb(s, k):
        for by, side, own, got in ((1, 0, 2, 1), (3, 1, 7, 0)):
            arrived(("x1", s, k, by), relay.at[s, side, k])
            total = part[s, k, own].astype(f32) + relay[s, side, k, got].astype(f32)
            comb_out[s, side, k] = total.astype(bf16)
            send(("x2", s, k, by), comb_out.at[s, side, k], comb_in.at[s, side, k], row_peer(by))

    def do_fin(s, k):
        a, m = places(s, k)
        for by, side in ((1, 0), (3, 1)):
            arrived(("x2", s, k, by), comb_in.at[s, side, k])
        for h in (0, 1):
            total = (
                own_part[s, k, h]
                + relay[s, 1 - h, k, 1 - h].astype(f32)
                + comb_in[s, h, k].astype(f32)
            )
            if s == 0:
                value, slope = gelu_pair(total)
                hidden[s, a, m, h] = value.astype(bf16)
                slopes[a, h] = slope
            else:
                hidden[s, a, m, h] = (total * slopes[m, h]).astype(bf16)
        block = hidden.at[s, a, m]
        for by in (1, 3):
            send(("a1", s, k, by), block, block, row_peer(by))

    def do_agf(s, k):
        a, m = places(s, k)
        for by, h in ((1, 0), (3, 1)):
            from_owner = turn(m, RING - by)
            arrived(("a1", s, k, by), hidden.at[s, a, from_owner])
            half = hidden.at[s, a, from_owner, h]
            send(("a2", s, k, by), half, half, row_peer(by))

    def do_om(s, k):
        a, m = places(s, k)
        for by, h in ((1, 0), (3, 1)):
            arrived(("a2", s, k, by), hidden.at[s, a, turn(m, 2), h])
        left = jnp.concatenate(
            [hidden[s, a, :, other].reshape(64, hid), hidden[s, a, :, d].reshape(64, hid)], axis=0
        )
        for n in range(width // BLOCK):
            tile = pl.ds(n * BLOCK, BLOCK)
            value = product_back(s, left, tile)
            pair_out[s, k, :, :, tile] = value[:64].astype(bf16).reshape(RING, 16, BLOCK)
            kept[s, k, :, :, tile] = value[64:].reshape(RING, 16, BLOCK)
        send(("p", s, k), pair_out.at[s, k], pair_in.at[s, k], sibling)

    def do_zs(s, k):
        arrived(("p", s, k), pair_in.at[s, k])
        total = kept[s, k] + pair_in[s, k].astype(f32)
        if k == 0:
            kept[s, k] = total
            return
        zsend[s, k] = total.astype(bf16)
        first, second = zsend.at[s, k, pl.ds(0, 2)], zsend.at[s, k, pl.ds(2, 2)]
        if k == 2:
            send(("z1", s, 1), first, zrelay.at[s, 0], major_peer(s, 1))
            send(("z1", s, 3), second, zrelay.at[s, 1], major_peer(s, 3))
        elif k == 1:
            send(("z0", s, 1), second, zown.at[s, 0], major_peer(s, 1))
        else:
            send(("z0", s, 3), first, zown.at[s, 1], major_peer(s, 3))

    def do_zc(s):
        for by, side, half in ((1, 0, 0), (3, 1, 2)):
            arrived(("z1", s, by), zrelay.at[s, side])
            total = zsend[s, by, pl.ds(half, 2)].astype(f32) + zrelay[s, side].astype(f32)
            zcomb_out[s, side] = total.astype(bf16)
            send(("z2", s, by), zcomb_out.at[s, side], zcomb_in.at[s, side], major_peer(s, by))

    def do_zf(s):
        for by, side in ((1, 0), (3, 1)):
            arrived(("z0", s, by), zown.at[s, side])
            arrived(("z2", s, by), zcomb_in.at[s, side])
        for h in (0, 1):
            rows = pl.ds(2 * h, 2)
            total = kept[s, 0, rows] + zown[s, 1 - h].astype(f32) + zcomb_in[s, h].astype(f32)
            fsend[s, rows] = total.astype(bf16)
            fown[s, rows] = total
        for by in (1, 3, 2):
            send(("f", s, by), fsend.at[s, turn(minor[s], by)], frecv.at[s, by - 1], minor_peer(s, by))

    stores = []

    def store(src, dst):
        copy = pltpu.make_async_copy(src, dst, local_sem.at[5 + len(stores)])
        copy.start()
        stores.append(copy)

    def do_yf(s):
        total = fown[s, minor[s]]
        for by in (1, 3, 2):
            arrived(("f", s, by), frecv.at[s, by - 1])
            total = total + frecv[s, by - 1].astype(f32)
        small[s] = total.astype(bf16)
        store(small.at[s], (out_h, gtok_h)[s])

    def do_tt():
        for a in range(RING):
            for n in range(width // BLOCK):
                tile = feats[0, a, :, :, :, pl.ds(n * BLOCK, BLOCK)].reshape(128, BLOCK)
                tok_t[pl.ds(n * BLOCK, BLOCK), pl.ds(a * 128, 128)] = tile.T

    def do_at():
        for a in range(RING):
            for n in range(hid // BLOCK):
                tile = hidden[0, a, :, :, :, pl.ds(n * BLOCK, BLOCK)].reshape(128, BLOCK)
                act_t[pl.ds(n * BLOCK, BLOCK), pl.ds(a * 128, 128)] = tile.T

    def swapped(ref, tile):
        return jnp.concatenate(
            [ref[1, b, a, :, :, tile].reshape(32, BLOCK) for a in range(RING) for b in range(RING)],
            axis=0,
        )

    def do_gdn():
        @pl.loop(0, width // BLOCK)
        def _(fb):
            tile = pl.ds(pl.multiple_of(fb * BLOCK, BLOCK), BLOCK)
            right = swapped(feats, tile)
            for hb in range(hid // BLOCK):
                rows = pl.ds(hb * BLOCK, BLOCK)
                value = jnp.dot(act_t[rows, :], right, preferred_element_type=f32)
                gdown_v[rows, tile] = (value * mask_at(1, hb, fb)).astype(bf16)

        store(gdown_v, gdown_h)

    def do_gup():
        for hb in range(hid // BLOCK):
            tile = pl.ds(hb * BLOCK, BLOCK)
            right = swapped(hidden, tile)

            @pl.loop(0, width // BLOCK)
            def _(fb):
                rows = pl.ds(pl.multiple_of(fb * BLOCK, BLOCK), BLOCK)
                value = jnp.dot(tok_t[rows, :], right, preferred_element_type=f32)
                gup_v[rows, tile] = (value * mask_at(0, hb, fb)).astype(bf16)

        store(gup_v, gup_h)

    steps = {
        "pass": do_pass, "last": do_last, "mm": do_mm, "comb": do_comb, "fin": do_fin, "agf": do_agf,
        "om": do_om, "zs": do_zs, "zc": do_zc, "zf": do_zf, "yf": do_yf,
        "tt": do_tt, "at": do_at, "gdn": do_gdn, "gup": do_gup,
    }
    for step in SCHEDULE:
        steps[step[0]](*step[1:])
    for copy in sent:
        copy.wait_send()
    for copy in stores:
        copy.wait()


def layer(tokens, up_weight, down_weight, grad_out, block_mask):
    rows, width = tokens.shape
    hid = up_weight.shape[1]
    bf16, f32 = jnp.bfloat16, jnp.float32
    V = pltpu.VMEM
    anywhere = pl.BlockSpec(memory_space=pl.ANY)
    return pl.pallas_call(
        kernel,
        out_shape=[
            jax.ShapeDtypeStruct((rows, width), bf16),
            jax.ShapeDtypeStruct((rows, width), bf16),
            jax.ShapeDtypeStruct((width, hid), bf16),
            jax.ShapeDtypeStruct((hid, width), bf16),
        ],
        in_specs=[anywhere] * 5,
        out_specs=[anywhere] * 4,
        scratch_shapes=[
            V((2, 4, 4, 2, 16, width), bf16),
            V((width, hid), bf16),
            V((hid, width), bf16),
            pltpu.SMEM(block_mask.shape, jnp.int32),
            V((2, 4, 8, 16, hid), bf16),
            V((2, 4, 2, 16, hid), f32),
            V((2, 2, 4, 2, 16, hid), bf16),
            V((2, 2, 4, 16, hid), bf16),
            V((2, 2, 4, 16, hid), bf16),
            V((4, 2, 16, hid), f32),
            V((2, 4, 4, 2, 16, hid), bf16),
            V((2, 4, 4, 16, width), bf16),
            V((2, 4, 4, 16, width), bf16),
            V((2, 4, 4, 16, width), f32),
            V((2, 4, 4, 16, width), bf16),
            V((2, 2, 2, 16, width), bf16),
            V((2, 2, 2, 16, width), bf16),
            V((2, 2, 2, 16, width), bf16),
            V((2, 2, 2, 16, width), bf16),
            V((2, 4, 16, width), bf16),
            V((2, 4, 16, width), f32),
            V((2, 3, 16, width), bf16),
            V((2, 16, width), bf16),
            V((width, 512), bf16),
            V((hid, 512), bf16),
            V((width, hid), bf16),
            V((hid, width), bf16),
            pltpu.SemaphoreType.DMA((120,)),
            pltpu.SemaphoreType.DMA((120,)),
            pltpu.SemaphoreType.DMA((9,)),
        ],
        compiler_params=pltpu.CompilerParams(
            collective_id=0, has_side_effects=True, vmem_limit_bytes=56 * 1024 * 1024
        ),
        cost_estimate=pl.CostEstimate(
            flops=12 * 512 * width * hid, bytes_accessed=8 * width * hid, transcendentals=0
        ),
    )(tokens, up_weight, down_weight, grad_out, block_mask)


def solution(mesh):
    in_specs = (
        P(("depth", "col"), "row"),
        P("row", ("col", "depth")),
        P(("col", "depth"), "row"),
        P(("depth", "col"), "row"),
        P(),
    )
    out_specs = (
        P(("depth", "col"), "row"),
        P(("depth", "col"), "row"),
        P("row", ("col", "depth")),
        P(("col", "depth"), "row"),
    )
    return jax.shard_map(layer, mesh=mesh, in_specs=in_specs, out_specs=out_specs, check_vma=False)
```

```python
import jax
import jax.numpy as jnp
from jax import lax
from jax.experimental import pallas as pl
from jax.experimental.pallas import tpu as pltpu
from jax.sharding import PartitionSpec as P

BLOCK = 256
RING = 4
MESH = pl.DeviceIdType.MESH

gelu_scale = 0.7978845608028654
gelu_cubic = 0.044715

SCHEDULE = (
    "own0", "own1", "mm00", "mm10", "comb00", "comb10", "pass0", "pass1", "fin00", "mm03", "mm01",
    "mm13", "last0", "last1", "comb03", "mm02", "mm12", "tt", "comb13", "fin03", "comb01",
    "comb02", "comb12", "mm11", "agf03", "fin02", "fin01", "fin12", "comb11", "om03", "agf02",
    "fin13", "agf12", "zs03", "fin11", "agf01", "om02", "agf13", "fin10", "om12", "agf11", "zs02",
    "om01", "zs12", "om13", "om11", "agf00", "zs01", "agf10", "zs13", "zc0", "zs11", "zc1", "om00",
    "om10", "at", "gup0", "zs00", "gup1", "gup2", "zs10", "zf0", "zf1", "gdn", "yf0", "yf1",
)


def gelu_pair(pre):
    inner = gelu_scale * (pre + gelu_cubic * pre * pre * pre)
    bend = jnp.tanh(inner)
    value = 0.5 * pre * (1.0 + bend)
    slope = 0.5 * (1.0 + bend) + 0.5 * pre * (1.0 - bend * bend) * gelu_scale * (
        1.0 + 3.0 * gelu_cubic * pre * pre
    )
    return value, slope


def kernel(
    tok_h, up_h, down_h, gout_h, mask_h,
    out_v, gtok_v, gup_v, gdown_v,
    feats, wu, wd, masks, part, own_part, relay, comb_out, comb_in, slopes, hidden,
    pair_out, pair_in, kept, zsend, zrelay, zown, zcomb_out, zcomb_in, fsend, fown, frecv,
    tok_t, act_t,
    send_sem, recv_sem, local_sem,
):
    f32, bf16 = jnp.float32, jnp.bfloat16
    width = wu.shape[0]
    hid = wu.shape[1]
    x = lax.axis_index("row")
    col = lax.axis_index("col")
    d = lax.axis_index("depth")
    z, y = lax.div(col, RING), lax.rem(col, RING)
    other = 1 - d
    major, minor = (z, y), (y, z)

    def turn(value, by):
        return lax.rem(value + by, RING)

    def major_peer(s, by):
        return {"col": turn(z, by) * RING + y} if s == 0 else {"col": z * RING + turn(y, by)}

    def minor_peer(s, by):
        return major_peer(1 - s, by)

    def row_peer(by):
        return {"row": turn(x, by)}

    sibling = {"depth": other}
    numbers = {}

    def remote(name, src, dst, peer):
        n = numbers.setdefault(name, len(numbers))
        return pltpu.make_async_remote_copy(
            src_ref=src, dst_ref=dst, send_sem=send_sem.at[n], recv_sem=recv_sem.at[n],
            device_id=peer, device_id_type=MESH,
        )

    sent = []

    def send(name, src, dst, peer):
        copy = remote(name, src, dst, peer)
        copy.start()
        sent.append(copy)

    def arrived(name, dst):
        remote(name, dst, dst, sibling).wait_recv()

    sources = (tok_h, gout_h)
    loads = [
        pltpu.make_async_copy(sources[0], feats.at[0, z, y, d], local_sem.at[0]),
        pltpu.make_async_copy(sources[1], feats.at[1, y, z, d], local_sem.at[1]),
        pltpu.make_async_copy(up_h, wu, local_sem.at[2]),
        pltpu.make_async_copy(mask_h, masks, local_sem.at[4]),
        pltpu.make_async_copy(down_h, wd, local_sem.at[3]),
    ]
    for load in loads:
        load.start()

    peers = [row_peer(1), row_peer(3), sibling]
    for by in (1, 2, 3):
        peers += [minor_peer(0, by), minor_peer(1, by)]
    barrier = pltpu.get_barrier_semaphore()
    for peer in peers:
        pl.semaphore_signal(barrier, inc=1, device_id=peer, device_id_type=MESH)
    pl.semaphore_wait(barrier, len(peers))

    hidden_corner = (col * 2 + d) * (hid // BLOCK)
    feature_corner = x * (width // BLOCK)

    def mask_at(which, hb, fb):
        return masks[which, feature_corner + fb, hidden_corner + hb].astype(f32)

    for s in (0, 1):
        for by in (1, 3, 2):
            send(("g1", s, by), sources[s], feats.at[s, major[s], minor[s], d], minor_peer(s, by))
    loads[3].wait()
    loads[2].wait()
    for fb in range(width // BLOCK):
        for hb in range(hid // BLOCK):
            tile = (pl.ds(fb * BLOCK, BLOCK), pl.ds(hb * BLOCK, BLOCK))
            wu[tile] = wu[tile] * mask_at(0, hb, fb).astype(bf16)
    loads[4].wait()
    for fb in range(width // BLOCK):
        for hb in range(hid // BLOCK):
            tile = (pl.ds(hb * BLOCK, BLOCK), pl.ds(fb * BLOCK, BLOCK))
            wd[tile] = wd[tile] * mask_at(1, hb, fb).astype(bf16)
    def do_own(s):
        loads[s].wait()
        for by in (1, 3, 2):
            arrived(("g1", s, by), feats.at[s, major[s], turn(minor[s], RING - by), d])
        mine = feats.at[s, major[s], :, d]
        send(("g2", s, 1), mine, mine, major_peer(s, 1))
        send(("g2", s, 3), mine, mine, major_peer(s, 3))
        send(("pair", s, 0), mine, mine, sibling)
    def do_pass(s):
        for by, half in ((1, 0), (3, 2)):
            a = turn(major[s], RING - by)
            whole = feats.at[s, a, :, d]
            arrived(("g2", s, by), whole)
            part_of = feats.at[s, a, pl.ds(half, 2), d]
            send(("g3", s, by), part_of, part_of, major_peer(s, by))
            send(("pair", s, RING - by), whole, whole, sibling)

    def do_last(s):
        a = turn(major[s], 2)
        for by, half in ((1, 0), (3, 2)):
            part_of = feats.at[s, a, pl.ds(half, 2), d]
            arrived(("g3", s, by), part_of)
            send(("pair2", s, by), part_of, part_of, sibling)

    def places(s, k):
        a = turn(major[s], k)
        return a, turn(x + RING - a, 0)

    def product(s, left, tile):
        if s == 0:
            return jnp.dot(left, wu[:, tile], preferred_element_type=f32)
        return lax.dot_general(
            left, wd[tile, :], (((1,), (1,)), ((), ())), preferred_element_type=f32
        )

    def product_back(s, left, tile):
        if s == 0:
            return jnp.dot(left, wd[:, tile], preferred_element_type=f32)
        return lax.dot_general(
            left, wu[tile, :], (((1,), (1,)), ((), ())), preferred_element_type=f32
        )

    def do_mm(s, k):
        a, m = places(s, k)
        if k == 2:
            for by, half in ((1, 0), (3, 2)):
                arrived(("pair2", s, by), feats.at[s, a, pl.ds(half, 2), other])
        else:
            arrived(("pair", s, k), feats.at[s, a, :, other])
        left = jnp.concatenate(
            [feats[s, a, turn(m, j)].reshape(32, width) for j in range(RING)], axis=0
        )
        for n in range(hid // BLOCK):
            tile = pl.ds(n * BLOCK, BLOCK)
            value = product(s, left, tile)
            part[s, k, :, :, tile] = value.astype(bf16).reshape(8, 16, BLOCK)
            own_part[s, k, :, :, tile] = value[:32].reshape(2, 16, BLOCK)
        send(("x1", s, k, 1), part.at[s, k, pl.ds(3, 2)], relay.at[s, 0, k], row_peer(1))
        send(("x1", s, k, 3), part.at[s, k, pl.ds(5, 2)], relay.at[s, 1, k], row_peer(3))

    def do_comb(s, k):
        for by, side, own, got in ((1, 0, 2, 1), (3, 1, 7, 0)):
            arrived(("x1", s, k, by), relay.at[s, side, k])
            total = part[s, k, own].astype(f32) + relay[s, side, k, got].astype(f32)
            comb_out[s, side, k] = total.astype(bf16)
            send(("x2", s, k, by), comb_out.at[s, side, k], comb_in.at[s, side, k], row_peer(by))

    def do_fin(s, k):
        a, m = places(s, k)
        for by, side in ((1, 0), (3, 1)):
            arrived(("x2", s, k, by), comb_in.at[s, side, k])
        for h in (0, 1):
            total = (
                own_part[s, k, h]
                + relay[s, 1 - h, k, 1 - h].astype(f32)
                + comb_in[s, h, k].astype(f32)
            )
            if s == 0:
                value, slope = gelu_pair(total)
                hidden[s, a, m, h] = value.astype(bf16)
                slopes[a, h] = slope
            else:
                hidden[s, a, m, h] = (total * slopes[m, h]).astype(bf16)
        block = hidden.at[s, a, m]
        for by in (1, 3):
            send(("a1", s, k, by), block, block, row_peer(by))

    def do_agf(s, k):
        a, m = places(s, k)
        for by, h in ((1, 0), (3, 1)):
            from_owner = turn(m, RING - by)
            arrived(("a1", s, k, by), hidden.at[s, a, from_owner])
            half = hidden.at[s, a, from_owner, h]
            send(("a2", s, k, by), half, half, row_peer(by))

    def do_om(s, k):
        a, m = places(s, k)
        for by, h in ((1, 0), (3, 1)):
            arrived(("a2", s, k, by), hidden.at[s, a, turn(m, 2), h])
        left = jnp.concatenate(
            [hidden[s, a, :, other].reshape(64, hid), hidden[s, a, :, d].reshape(64, hid)], axis=0
        )
        for n in range(width // BLOCK):
            tile = pl.ds(n * BLOCK, BLOCK)
            value = product_back(s, left, tile)
            pair_out[s, k, :, :, tile] = value[:64].astype(bf16).reshape(RING, 16, BLOCK)
            kept[s, k, :, :, tile] = value[64:].reshape(RING, 16, BLOCK)
        send(("p", s, k), pair_out.at[s, k], pair_in.at[s, k], sibling)

    def do_zs(s, k):
        arrived(("p", s, k), pair_in.at[s, k])
        total = kept[s, k] + pair_in[s, k].astype(f32)
        if k == 0:
            kept[s, k] = total
            return
        zsend[s, k] = total.astype(bf16)
        first, second = zsend.at[s, k, pl.ds(0, 2)], zsend.at[s, k, pl.ds(2, 2)]
        if k == 2:
            send(("z1", s, 1), first, zrelay.at[s, 0], major_peer(s, 1))
            send(("z1", s, 3), second, zrelay.at[s, 1], major_peer(s, 3))
        elif k == 1:
            send(("z0", s, 1), second, zown.at[s, 0], major_peer(s, 1))
        else:
            send(("z0", s, 3), first, zown.at[s, 1], major_peer(s, 3))

    def do_zc(s):
        for by, side, half in ((1, 0, 0), (3, 1, 2)):
            arrived(("z1", s, by), zrelay.at[s, side])
            total = zsend[s, by, pl.ds(half, 2)].astype(f32) + zrelay[s, side].astype(f32)
            zcomb_out[s, side] = total.astype(bf16)
            send(("z2", s, by), zcomb_out.at[s, side], zcomb_in.at[s, side], major_peer(s, by))

    def do_zf(s):
        for by, side in ((1, 0), (3, 1)):
            arrived(("z0", s, by), zown.at[s, side])
            arrived(("z2", s, by), zcomb_in.at[s, side])
        for h in (0, 1):
            rows = pl.ds(2 * h, 2)
            total = kept[s, 0, rows] + zown[s, 1 - h].astype(f32) + zcomb_in[s, h].astype(f32)
            fsend[s, rows] = total.astype(bf16)
            fown[s, rows] = total
        for by in (1, 3, 2):
            send(("f", s, by), fsend.at[s, turn(minor[s], by)], frecv.at[s, by - 1], minor_peer(s, by))

    def do_yf(s):
        total = fown[s, minor[s]]
        for by in (1, 3, 2):
            arrived(("f", s, by), frecv.at[s, by - 1])
            total = total + frecv[s, by - 1].astype(f32)
        (out_v, gtok_v)[s][...] = total.astype(bf16)

    def do_tt():
        for a in range(RING):
            for n in range(width // BLOCK):
                tile = feats[0, a, :, :, :, pl.ds(n * BLOCK, BLOCK)].reshape(128, BLOCK)
                tok_t[pl.ds(n * BLOCK, BLOCK), pl.ds(a * 128, 128)] = tile.T

    def do_at():
        for a in range(RING):
            for n in range(hid // BLOCK):
                tile = hidden[0, a, :, :, :, pl.ds(n * BLOCK, BLOCK)].reshape(128, BLOCK)
                act_t[pl.ds(n * BLOCK, BLOCK), pl.ds(a * 128, 128)] = tile.T

    def swapped(ref, tile):
        return jnp.concatenate(
            [ref[1, b, a, :, :, tile].reshape(32, BLOCK) for a in range(RING) for b in range(RING)],
            axis=0,
        )

    def do_gdn():
        @pl.loop(0, width // BLOCK)
        def _(fb):
            tile = pl.ds(pl.multiple_of(fb * BLOCK, BLOCK), BLOCK)
            right = swapped(feats, tile)
            for hb in range(hid // BLOCK):
                rows = pl.ds(hb * BLOCK, BLOCK)
                value = jnp.dot(act_t[rows, :], right, preferred_element_type=f32)
                gdown_v[rows, tile] = (value * mask_at(1, hb, fb)).astype(bf16)

    def do_gup(hb):
        tile = pl.ds(hb * BLOCK, BLOCK)
        right = swapped(hidden, tile)

        for half in (0, 1):
            rows = pl.ds(half * (width // 2), width // 2)
            value = jnp.dot(tok_t[rows, :], right, preferred_element_type=f32)
            for n in range(width // 2 // BLOCK):
                fb = half * (width // 2 // BLOCK) + n
                gup_v[pl.ds(fb * BLOCK, BLOCK), tile] = (
                    value[n * BLOCK : (n + 1) * BLOCK] * mask_at(0, hb, fb)
                ).astype(bf16)

    steps = {
        "own": do_own, "pass": do_pass, "last": do_last, "mm": do_mm, "comb": do_comb, "fin": do_fin, "agf": do_agf,
        "om": do_om, "zs": do_zs, "zc": do_zc, "zf": do_zf, "yf": do_yf,
        "tt": do_tt, "at": do_at, "gdn": do_gdn, "gup": do_gup,
    }
    for step in SCHEDULE:
        name = step.rstrip("0123")
        steps[name](*[int(v) for v in step[len(name):]])
    for copy in sent:
        copy.wait_send()


def write_out(*refs):
    sources, targets, sems = refs[:4], refs[4:8], refs[8]
    copies = [pltpu.make_async_copy(a, b, sems.at[i]) for i, (a, b) in enumerate(zip(sources, targets))]
    for copy in copies:
        copy.start()
    for copy in copies:
        copy.wait()


def layer(tokens, up_weight, down_weight, grad_out, block_mask):
    rows, width = tokens.shape
    hid = up_weight.shape[1]
    bf16, f32 = jnp.bfloat16, jnp.float32
    V = pltpu.VMEM
    anywhere = pl.BlockSpec(memory_space=pl.ANY)
    block_mask = jnp.transpose(block_mask, (0, 2, 1))
    operands = (tokens, up_weight, down_weight, grad_out, block_mask)
    shapes = ((rows, width), (rows, width), (width, hid), (hid, width))
    results = pl.pallas_call(
        kernel,
        out_shape=[V(shape, bf16) for shape in shapes],
        in_specs=[pl.BlockSpec(memory_space=pltpu.HBM)] * 5,
        out_specs=[pl.BlockSpec(memory_space=V)] * 4,
        scratch_shapes=[
            V((2, 4, 4, 2, 16, width), bf16),
            V((width, hid), bf16),
            V((hid, width), bf16),
            pltpu.SMEM(block_mask.shape, jnp.int32),
            V((2, 4, 8, 16, hid), bf16),
            V((2, 4, 2, 16, hid), f32),
            V((2, 2, 4, 2, 16, hid), bf16),
            V((2, 2, 4, 16, hid), bf16),
            V((2, 2, 4, 16, hid), bf16),
            V((4, 2, 16, hid), f32),
            V((2, 4, 4, 2, 16, hid), bf16),
            V((2, 4, 4, 16, width), bf16),
            V((2, 4, 4, 16, width), bf16),
            V((2, 4, 4, 16, width), f32),
            V((2, 4, 4, 16, width), bf16),
            V((2, 2, 2, 16, width), bf16),
            V((2, 2, 2, 16, width), bf16),
            V((2, 2, 2, 16, width), bf16),
            V((2, 2, 2, 16, width), bf16),
            V((2, 4, 16, width), bf16),
            V((2, 4, 16, width), f32),
            V((2, 3, 16, width), bf16),
            V((width, 512), bf16),
            V((hid, 512), bf16),
            pltpu.SemaphoreType.DMA((120,)),
            pltpu.SemaphoreType.DMA((120,)),
            pltpu.SemaphoreType.DMA((5,)),
        ],
        compiler_params=pltpu.CompilerParams(
            collective_id=0, has_side_effects=True, vmem_limit_bytes=44 * 1024 * 1024
        ),
        cost_estimate=pl.CostEstimate(
            flops=12 * 512 * width * hid, bytes_accessed=8 * width * hid, transcendentals=0
        ),
    )(*[pltpu.with_memory_space_constraint(v, pltpu.HBM) for v in operands])
    return pl.pallas_call(
        write_out,
        out_shape=[jax.ShapeDtypeStruct(shape, bf16) for shape in shapes],
        in_specs=[anywhere] * 4,
        out_specs=[anywhere] * 4,
        scratch_shapes=[pltpu.SemaphoreType.DMA((4,))],
        compiler_params=pltpu.CompilerParams(vmem_limit_bytes=1024 * 1024),
    )(*results)


def solution(mesh):
    in_specs = (
        P(("depth", "col"), "row"),
        P("row", ("col", "depth")),
        P(("col", "depth"), "row"),
        P(("depth", "col"), "row"),
        P(),
    )
    out_specs = (
        P(("depth", "col"), "row"),
        P(("depth", "col"), "row"),
        P("row", ("col", "depth")),
        P(("col", "depth"), "row"),
    )
    return jax.shard_map(layer, mesh=mesh, in_specs=in_specs, out_specs=out_specs, check_vma=False)
```

```python
import jax
import jax.numpy as jnp
from jax import lax
from jax.experimental import pallas as pl
from jax.experimental.pallas import tpu as pltpu
from jax.sharding import PartitionSpec as P

BLOCK = 256
RING = 4
SEMS = 192
MESH = pl.DeviceIdType.MESH

gelu_scale = 0.7978845608028654
gelu_cubic = 0.044715

SCHEDULE = (
    "own0", "own1", "far1", "far0", "mm00", "mm10", "pass0", "pass1", "comb00", "mm03", "mm01",
    "mm11", "mm13", "last0", "last1", "comb03", "mm02", "mm12", "comb01", "comb11", "tt", "comb13",
    "comb02", "fin00", "comb12", "fin03", "fin02", "fin01", "fin12", "fin11", "agf02", "fin13",
    "agf12", "comb10", "agf11", "agf03", "agf01", "om02", "agf13", "agf00", "om12", "fin10",
    "zs02", "om11", "om03", "zs12", "om01", "om13", "om00", "zs03", "zs01", "zs11", "agf10",
    "zs13", "zc00", "at", "zc01", "zs00", "zc10", "zc11", "om10", "gup1", "gup0", "zs10", "zf00",
    "zf10", "gup2", "zf01", "zf11", "gdn", "yf0", "yf1",
)


def gelu_pair(pre):
    inner = gelu_scale * (pre + gelu_cubic * pre * pre * pre)
    bend = jnp.tanh(inner)
    value = 0.5 * pre * (1.0 + bend)
    slope = 0.5 * (1.0 + bend) + 0.5 * pre * (1.0 - bend * bend) * gelu_scale * (
        1.0 + 3.0 * gelu_cubic * pre * pre
    )
    return value, slope


def kernel(
    tok_h, up_h, down_h, gout_h, mask_h,
    out_v, gtok_v, gup_v, gdown_v,
    feats, wu, wd, masks, part, own_part, relay, comb_out, comb_in, slopes, hidden,
    pair_out, pair_in, kept, zsend, zrelay, zown, zcomb_out, zcomb_in, fsend, fown, frecv,
    tok_t, act_t,
    send_sem, recv_sem, local_sem,
):
    f32, bf16 = jnp.float32, jnp.bfloat16
    width = wu.shape[0]
    hid = wu.shape[1]
    x = lax.axis_index("row")
    col = lax.axis_index("col")
    d = lax.axis_index("depth")
    z, y = lax.div(col, RING), lax.rem(col, RING)
    other = 1 - d
    major, minor = (z, y), (y, z)

    def turn(value, by):
        return lax.rem(value + by, RING)

    def major_peer(s, by):
        return {"col": turn(z, by) * RING + y} if s == 0 else {"col": z * RING + turn(y, by)}

    def minor_peer(s, by):
        return major_peer(1 - s, by)

    def row_peer(by):
        return {"row": turn(x, by)}

    sibling = {"depth": other}
    columns = (pl.ds(0, width // 2), pl.ds(width // 2, width // 2))
    numbers = {}

    def remote(name, src, dst, peer):
        n = numbers.setdefault(name, len(numbers))
        return pltpu.make_async_remote_copy(
            src_ref=src, dst_ref=dst, send_sem=send_sem.at[n], recv_sem=recv_sem.at[n],
            device_id=peer, device_id_type=MESH,
        )

    sent = []

    def send(name, src, dst, peer):
        copy = remote(name, src, dst, peer)
        copy.start()
        sent.append(copy)

    def arrived(name, dst):
        remote(name, dst, dst, sibling).wait_recv()

    sources = (tok_h, gout_h)
    peers = [row_peer(1), row_peer(3), sibling]
    for by in (1, 2, 3):
        peers += [minor_peer(0, by), minor_peer(1, by)]
    barrier = pltpu.get_barrier_semaphore()
    for peer in peers:
        pl.semaphore_signal(barrier, inc=1, device_id=peer, device_id_type=MESH)
    loads = [
        pltpu.make_async_copy(sources[0], feats.at[0, z, y, d], local_sem.at[0]),
        pltpu.make_async_copy(sources[1], feats.at[1, y, z, d], local_sem.at[1]),
        pltpu.make_async_copy(up_h, wu, local_sem.at[2]),
        pltpu.make_async_copy(mask_h, masks, local_sem.at[4]),
        pltpu.make_async_copy(down_h, wd, local_sem.at[3]),
    ]
    for load in loads:
        load.start()
    pl.semaphore_wait(barrier, len(peers))

    hidden_corner = (col * 2 + d) * (hid // BLOCK)
    feature_corner = x * (width // BLOCK)

    def mask_at(which, hb, fb):
        return masks[which, feature_corner + fb, hidden_corner + hb].astype(f32)

    def here(s, a, m, count=None):
        place = m if count is None else pl.ds(m, count)
        return feats.at[s, a, place, d]

    for s in (0, 1):
        for by in (1, 3, 2):
            send(("g1", s, by), sources[s], here(s, major[s], minor[s]), minor_peer(s, by))
    for s in (0, 1):
        mine = here(s, major[s], minor[s])
        for by in (1, 3):
            send(("g2", s, by, 0), sources[s], mine, major_peer(s, by))
        send(("pair", s, 0, 0), sources[s], mine, sibling)

    loads[3].wait()
    loads[2].wait()
    for fb in range(width // BLOCK):
        for hb in range(hid // BLOCK):
            tile = (pl.ds(fb * BLOCK, BLOCK), pl.ds(hb * BLOCK, BLOCK))
            wu[tile] = wu[tile] * mask_at(0, hb, fb).astype(bf16)
    loads[4].wait()
    for fb in range(width // BLOCK):
        for hb in range(hid // BLOCK):
            tile = (pl.ds(hb * BLOCK, BLOCK), pl.ds(fb * BLOCK, BLOCK))
            wd[tile] = wd[tile] * mask_at(1, hb, fb).astype(bf16)
    def pass_on(s, steps):
        for step in steps:
            m = turn(minor[s], RING - step)
            block = here(s, major[s], m)
            arrived(("g1", s, step), block)
            for by in (1, 3):
                send(("g2", s, by, step), block, block, major_peer(s, by))
            send(("pair", s, 0, step), block, block, sibling)

    def do_own(s):
        pass_on(s, (1, 3))

    def do_far(s):
        pass_on(s, (2,))
        loads[s].wait()

    def do_pass(s):
        for step in (0, 1, 3, 2):
            for by in (1, 3):
                m = turn(minor[s], RING - step)
                block = here(s, turn(major[s], RING - by), m)
                arrived(("g2", s, by, step), block)
        for by, half in ((1, 0), (3, 2)):
            a = turn(major[s], RING - by)
            part_of = here(s, a, half, 2)
            send(("g3", s, by), part_of, part_of, major_peer(s, by))
            whole = here(s, a, 0, RING)
            send(("pair", s, RING - by), whole, whole, sibling)

    def do_last(s):
        a = turn(major[s], 2)
        for by, half in ((1, 0), (3, 2)):
            part_of = here(s, a, half, 2)
            arrived(("g3", s, by), part_of)
            send(("pair2", s, by), part_of, part_of, sibling)

    def places(s, k):
        a = turn(major[s], k)
        return a, turn(x + RING - a, 0)

    def product(s, left, tile):
        if s == 0:
            return jnp.dot(left, wu[:, tile], preferred_element_type=f32)
        return lax.dot_general(
            left, wd[tile, :], (((1,), (1,)), ((), ())), preferred_element_type=f32
        )

    def product_back(s, left, tile):
        if s == 0:
            return jnp.dot(left, wd[:, tile], preferred_element_type=f32)
        return lax.dot_general(
            left, wu[tile, :], (((1,), (1,)), ((), ())), preferred_element_type=f32
        )

    def do_mm(s, k):
        a, m = places(s, k)
        if k == 2:
            for by, half in ((1, 0), (3, 2)):
                arrived(("pair2", s, by), feats.at[s, a, pl.ds(half, 2), other])
        elif k == 0:
            for step in range(RING):
                block = feats.at[s, a, turn(minor[s], RING - step), other]
                arrived(("pair", s, 0, step), block)
        else:
            arrived(("pair", s, k), feats.at[s, a, :, other])
        left = jnp.concatenate(
            [feats[s, a, turn(m, j)].reshape(32, width) for j in range(RING)], axis=0
        )
        for n in range(hid // BLOCK):
            tile = pl.ds(n * BLOCK, BLOCK)
            value = product(s, left, tile)
            part[s, k, :, :, tile] = value.astype(bf16).reshape(8, 16, BLOCK)
            own_part[s, k, :, :, tile] = value[:32].reshape(2, 16, BLOCK)
        send(("x1", s, k, 1), part.at[s, k, pl.ds(3, 2)], relay.at[s, 0, k], row_peer(1))
        send(("x1", s, k, 3), part.at[s, k, pl.ds(5, 2)], relay.at[s, 1, k], row_peer(3))

    def do_comb(s, k):
        for by, side, own, got in ((1, 0, 2, 1), (3, 1, 7, 0)):
            arrived(("x1", s, k, by), relay.at[s, side, k])
            total = part[s, k, own].astype(f32) + relay[s, side, k, got].astype(f32)
            comb_out[s, side, k] = total.astype(bf16)
            send(("x2", s, k, by), comb_out.at[s, side, k], comb_in.at[s, side, k], row_peer(by))

    def do_fin(s, k):
        a, m = places(s, k)
        for by, side in ((1, 0), (3, 1)):
            arrived(("x2", s, k, by), comb_in.at[s, side, k])
        for h in (0, 1):
            total = (
                own_part[s, k, h]
                + relay[s, 1 - h, k, 1 - h].astype(f32)
                + comb_in[s, h, k].astype(f32)
            )
            if s == 0:
                value, slope = gelu_pair(total)
                hidden[s, a, m, h] = value.astype(bf16)
                slopes[a, h] = slope
            else:
                hidden[s, a, m, h] = (total * slopes[m, h]).astype(bf16)
        block = hidden.at[s, a, m]
        for by in (1, 3):
            send(("a1", s, k, by), block, block, row_peer(by))

    def do_agf(s, k):
        a, m = places(s, k)
        for by, h in ((1, 0), (3, 1)):
            from_owner = turn(m, RING - by)
            arrived(("a1", s, k, by), hidden.at[s, a, from_owner])
            half = hidden.at[s, a, from_owner, h]
            send(("a2", s, k, by), half, half, row_peer(by))

    def do_om(s, k):
        a, m = places(s, k)
        for by, h in ((1, 0), (3, 1)):
            arrived(("a2", s, k, by), hidden.at[s, a, turn(m, 2), h])
        left = jnp.concatenate(
            [hidden[s, a, :, other].reshape(64, hid), hidden[s, a, :, d].reshape(64, hid)], axis=0
        )
        for n in range(width // BLOCK):
            tile = pl.ds(n * BLOCK, BLOCK)
            value = product_back(s, left, tile)
            pair_out[s, k, :, :, tile] = value[:64].astype(bf16).reshape(RING, 16, BLOCK)
            kept[s, k, :, :, tile] = value[64:].reshape(RING, 16, BLOCK)
        send(("p", s, k), pair_out.at[s, k], pair_in.at[s, k], sibling)

    def do_zs(s, k):
        arrived(("p", s, k), pair_in.at[s, k])
        total = kept[s, k] + pair_in[s, k].astype(f32)
        if k == 0:
            kept[s, k] = total
            return
        zsend[s, k] = total.astype(bf16)
        for h in (0, 1):
            first, second = zsend.at[s, k, pl.ds(0, 2), :, columns[h]], zsend.at[s, k, pl.ds(2, 2), :, columns[h]]
            if k == 2:
                send(("z1", s, 1, h), first, zrelay.at[s, 0, :, :, columns[h]], major_peer(s, 1))
                send(("z1", s, 3, h), second, zrelay.at[s, 1, :, :, columns[h]], major_peer(s, 3))
            elif k == 1:
                send(("z0", s, 1, h), second, zown.at[s, 0, :, :, columns[h]], major_peer(s, 1))
            else:
                send(("z0", s, 3, h), first, zown.at[s, 1, :, :, columns[h]], major_peer(s, 3))

    def do_zc(s, h):
        for by, side, half in ((1, 0, 0), (3, 1, 2)):
            where = (s, side, slice(None), slice(None), columns[h])
            arrived(("z1", s, by, h), zrelay.at[where])
            total = zsend[s, by, pl.ds(half, 2), :, columns[h]].astype(f32) + zrelay[where].astype(f32)
            zcomb_out[where] = total.astype(bf16)
            send(("z2", s, by, h), zcomb_out.at[where], zcomb_in.at[where], major_peer(s, by))

    def do_zf(s, h):
        cols = columns[h]
        for by, side in ((1, 0), (3, 1)):
            arrived(("z0", s, by, h), zown.at[s, side, :, :, cols])
            arrived(("z2", s, by, h), zcomb_in.at[s, side, :, :, cols])
        for g in (0, 1):
            rows = pl.ds(2 * g, 2)
            total = (
                kept[s, 0, rows, :, cols]
                + zown[s, 1 - g, :, :, cols].astype(f32)
                + zcomb_in[s, g, :, :, cols].astype(f32)
            )
            fsend[s, rows, :, cols] = total.astype(bf16)
            fown[s, rows, :, cols] = total
        for by in (1, 3, 2):
            block = fsend.at[s, turn(minor[s], by), :, cols]
            send(("f", s, by, h), block, frecv.at[s, by - 1, :, cols], minor_peer(s, by))

    def do_yf(s):
        for h in (0, 1):
            cols = columns[h]
            total = fown[s, minor[s], :, cols]
            for by in (1, 3, 2):
                arrived(("f", s, by, h), frecv.at[s, by - 1, :, cols])
                total = total + frecv[s, by - 1, :, cols].astype(f32)
            (out_v, gtok_v)[s][:, cols] = total.astype(bf16)

    def do_tt():
        for a in range(RING):
            for n in range(width // BLOCK):
                tile = feats[0, a, :, :, :, pl.ds(n * BLOCK, BLOCK)].reshape(128, BLOCK)
                tok_t[pl.ds(n * BLOCK, BLOCK), pl.ds(a * 128, 128)] = tile.T

    def do_at():
        for a in range(RING):
            for n in range(hid // BLOCK):
                tile = hidden[0, a, :, :, :, pl.ds(n * BLOCK, BLOCK)].reshape(128, BLOCK)
                act_t[pl.ds(n * BLOCK, BLOCK), pl.ds(a * 128, 128)] = tile.T

    def swapped(ref, tile):
        return jnp.concatenate(
            [ref[1, b, a, :, :, tile].reshape(32, BLOCK) for a in range(RING) for b in range(RING)],
            axis=0,
        )

    def do_gdn():
        @pl.loop(0, width // BLOCK)
        def _(fb):
            tile = pl.ds(pl.multiple_of(fb * BLOCK, BLOCK), BLOCK)
            right = swapped(feats, tile)
            for hb in range(hid // BLOCK):
                rows = pl.ds(hb * BLOCK, BLOCK)
                value = jnp.dot(act_t[rows, :], right, preferred_element_type=f32)
                gdown_v[rows, tile] = (value * mask_at(1, hb, fb)).astype(bf16)

    def do_gup(hb):
        tile = pl.ds(hb * BLOCK, BLOCK)
        right = swapped(hidden, tile)

        for half in (0, 1):
            rows = pl.ds(half * (width // 2), width // 2)
            value = jnp.dot(tok_t[rows, :], right, preferred_element_type=f32)
            for n in range(width // 2 // BLOCK):
                fb = half * (width // 2 // BLOCK) + n
                gup_v[pl.ds(fb * BLOCK, BLOCK), tile] = (
                    value[n * BLOCK : (n + 1) * BLOCK] * mask_at(0, hb, fb)
                ).astype(bf16)

    steps = {
        "own": do_own, "far": do_far, "pass": do_pass, "last": do_last, "mm": do_mm, "comb": do_comb, "fin": do_fin, "agf": do_agf,
        "om": do_om, "zs": do_zs, "zc": do_zc, "zf": do_zf, "yf": do_yf,
        "tt": do_tt, "at": do_at, "gdn": do_gdn, "gup": do_gup,
    }
    for step in SCHEDULE:
        name = step.rstrip("0123")
        steps[name](*[int(v) for v in step[len(name):]])
    for copy in sent:
        copy.wait_send()


def write_out(*refs):
    sources, targets, sems = refs[:4], refs[4:8], refs[8]
    copies = [pltpu.make_async_copy(a, b, sems.at[i]) for i, (a, b) in enumerate(zip(sources, targets))]
    for copy in copies:
        copy.start()
    for copy in copies:
        copy.wait()


def layer(tokens, up_weight, down_weight, grad_out, block_mask):
    rows, width = tokens.shape
    hid = up_weight.shape[1]
    bf16, f32 = jnp.bfloat16, jnp.float32
    V = pltpu.VMEM
    anywhere = pl.BlockSpec(memory_space=pl.ANY)
    block_mask = jnp.transpose(block_mask, (0, 2, 1))
    operands = (tokens, up_weight, down_weight, grad_out, block_mask)
    shapes = ((rows, width), (rows, width), (width, hid), (hid, width))
    results = pl.pallas_call(
        kernel,
        out_shape=[V(shape, bf16) for shape in shapes],
        in_specs=[pl.BlockSpec(memory_space=pltpu.HBM)] * 5,
        out_specs=[pl.BlockSpec(memory_space=V)] * 4,
        scratch_shapes=[
            V((2, 4, 4, 2, 16, width), bf16),
            V((width, hid), bf16),
            V((hid, width), bf16),
            pltpu.SMEM(block_mask.shape, jnp.int32),
            V((2, 4, 8, 16, hid), bf16),
            V((2, 4, 2, 16, hid), f32),
            V((2, 2, 4, 2, 16, hid), bf16),
            V((2, 2, 4, 16, hid), bf16),
            V((2, 2, 4, 16, hid), bf16),
            V((4, 2, 16, hid), f32),
            V((2, 4, 4, 2, 16, hid), bf16),
            V((2, 4, 4, 16, width), bf16),
            V((2, 4, 4, 16, width), bf16),
            V((2, 4, 4, 16, width), f32),
            V((2, 4, 4, 16, width), bf16),
            V((2, 2, 2, 16, width), bf16),
            V((2, 2, 2, 16, width), bf16),
            V((2, 2, 2, 16, width), bf16),
            V((2, 2, 2, 16, width), bf16),
            V((2, 4, 16, width), bf16),
            V((2, 4, 16, width), f32),
            V((2, 3, 16, width), bf16),
            V((width, 512), bf16),
            V((hid, 512), bf16),
            pltpu.SemaphoreType.DMA((SEMS,)),
            pltpu.SemaphoreType.DMA((SEMS,)),
            pltpu.SemaphoreType.DMA((5,)),
        ],
        compiler_params=pltpu.CompilerParams(
            collective_id=0, has_side_effects=True, vmem_limit_bytes=44 * 1024 * 1024
        ),
        cost_estimate=pl.CostEstimate(
            flops=12 * 512 * width * hid, bytes_accessed=8 * width * hid, transcendentals=0
        ),
    )(*[pltpu.with_memory_space_constraint(v, pltpu.HBM) for v in operands])
    return pl.pallas_call(
        write_out,
        out_shape=[jax.ShapeDtypeStruct(shape, bf16) for shape in shapes],
        in_specs=[anywhere] * 4,
        out_specs=[anywhere] * 4,
        scratch_shapes=[pltpu.SemaphoreType.DMA((4,))],
        compiler_params=pltpu.CompilerParams(vmem_limit_bytes=1024 * 1024),
    )(*results)


def solution(mesh):
    in_specs = (
        P(("depth", "col"), "row"),
        P("row", ("col", "depth")),
        P(("col", "depth"), "row"),
        P(("depth", "col"), "row"),
        P(),
    )
    out_specs = (
        P(("depth", "col"), "row"),
        P(("depth", "col"), "row"),
        P("row", ("col", "depth")),
        P(("col", "depth"), "row"),
    )
    return jax.shard_map(layer, mesh=mesh, in_specs=in_specs, out_specs=out_specs, check_vma=False)
```

```python
import jax
import jax.numpy as jnp
from jax import lax
from jax.experimental import pallas as pl
from jax.experimental.pallas import tpu as pltpu
from jax.sharding import PartitionSpec as P

BLOCK = 256
RING = 4
SEMS = 192
DIRECT_SUMS = ((0, 0), (1, 0))
DIRECT = ((1, 0), (1, 2))
MESH = pl.DeviceIdType.MESH

gelu_scale = 0.7978845608028654
gelu_cubic = 0.044715

SCHEDULE = (
    "mask0", "own0", "own1", "mask1", "far0", "far1", "mm00", "mm10", "early0", "pass0", "early1",
    "mm01", "pass1", "mm03", "mm11", "last0", "mm13", "last1", "mm02", "tt", "fin00", "comb01",
    "comb03", "mm12", "comb02", "comb13", "comb11", "fin01", "fin03", "fin02", "fin11", "comb12",
    "fin13", "agf01", "agf11", "agf03", "agf02", "agf13", "fin12", "agf00", "om01", "om11", "zs01",
    "fin10", "om02", "om03", "zs11", "om13", "zs02", "zs13", "om12", "om00", "zs03", "zs12",
    "om10", "zs00", "yg11", "yg02", "gup2", "at", "zs10", "yg13", "gup0", "yg01", "yg03", "gup1",
    "yg12", "yg00", "gdn", "yg10", "yf1", "yf0",
)


def gelu_pair(pre):
    inner = gelu_scale * (pre + gelu_cubic * pre * pre * pre)
    bend = jnp.tanh(inner)
    value = 0.5 * pre * (1.0 + bend)
    slope = 0.5 * (1.0 + bend) + 0.5 * pre * (1.0 - bend * bend) * gelu_scale * (
        1.0 + 3.0 * gelu_cubic * pre * pre
    )
    return value, slope


def kernel(
    tok_h, up_h, down_h, gout_h, mask_h,
    out_v, gtok_v, gup_v, gdown_v,
    feats, wu, wd, masks, part, own_part, relay, comb_out, comb_in, slopes, hidden,
    pair_out, pair_in, kept, ysend, yrecv, fsend, fown, frecv,
    straight, tok_t, act_t,
    send_sem, recv_sem, local_sem,
):
    f32, bf16 = jnp.float32, jnp.bfloat16
    width = wu.shape[0]
    hid = wu.shape[1]
    x = lax.axis_index("row")
    col = lax.axis_index("col")
    d = lax.axis_index("depth")
    z, y = lax.div(col, RING), lax.rem(col, RING)
    other = 1 - d
    major, minor = (z, y), (y, z)

    def turn(value, by):
        return lax.rem(value + by, RING)

    def major_peer(s, by):
        return {"col": turn(z, by) * RING + y} if s == 0 else {"col": z * RING + turn(y, by)}

    def minor_peer(s, by):
        return major_peer(1 - s, by)

    def row_peer(by):
        return {"row": turn(x, by)}

    sibling = {"depth": other}
    numbers = {}

    def remote(name, src, dst, peer):
        n = numbers.setdefault(name, len(numbers))
        return pltpu.make_async_remote_copy(
            src_ref=src, dst_ref=dst, send_sem=send_sem.at[n], recv_sem=recv_sem.at[n],
            device_id=peer, device_id_type=MESH,
        )

    sent = []

    def send(name, src, dst, peer):
        copy = remote(name, src, dst, peer)
        copy.start()
        sent.append(copy)

    def arrived(name, dst):
        remote(name, dst, dst, sibling).wait_recv()

    sources = (tok_h, gout_h)
    peers = [row_peer(1), row_peer(2), row_peer(3), sibling]
    for by in (1, 2, 3):
        peers += [minor_peer(0, by), minor_peer(1, by)]
    barrier = pltpu.get_barrier_semaphore()
    for peer in peers:
        pl.semaphore_signal(barrier, inc=1, device_id=peer, device_id_type=MESH)
    loads = [
        pltpu.make_async_copy(sources[0], feats.at[0, z, y, d], local_sem.at[0]),
        pltpu.make_async_copy(sources[1], feats.at[1, y, z, d], local_sem.at[1]),
        pltpu.make_async_copy(up_h, wu, local_sem.at[2]),
        pltpu.make_async_copy(mask_h, masks, local_sem.at[4]),
        pltpu.make_async_copy(down_h, wd, local_sem.at[3]),
    ]
    for n in (0, 1, 3):
        loads[n].start()
    pl.semaphore_wait(barrier, len(peers))

    hidden_corner = (col * 2 + d) * (hid // BLOCK)
    feature_corner = x * (width // BLOCK)

    def mask_at(which, hb, fb):
        return masks[which, feature_corner + fb, hidden_corner + hb].astype(f32)

    def here(s, a, m):
        return feats.at[s, a, m, d]

    for s in (0, 1):
        for by in (1, 3, 2):
            send(("g1", s, by), sources[s], here(s, major[s], minor[s]), minor_peer(s, by))
    for s in (0, 1):
        mine = here(s, major[s], minor[s])
        for by in (1, 3):
            send(("g2", s, by, 0), sources[s], mine, major_peer(s, by))
        send(("pair", s, 0, 0), sources[s], mine, sibling)

    loads[2].start()
    loads[4].start()
    loads[3].wait()

    def do_mask(which):
        loads[(2, 4)[which]].wait()
        for fb in range(width // BLOCK):
            for hb in range(hid // BLOCK):
                features, units = pl.ds(fb * BLOCK, BLOCK), pl.ds(hb * BLOCK, BLOCK)
                held, tile = ((wu, (features, units)), (wd, (units, features)))[which]
                held[tile] = held[tile] * mask_at(which, hb, fb).astype(bf16)

    def pass_on(s, steps):
        for step in steps:
            m = turn(minor[s], RING - step)
            block = here(s, major[s], m)
            arrived(("g1", s, step), block)
            for by in (1, 3):
                send(("g2", s, by, step), block, block, major_peer(s, by))
            send(("pair", s, 0, step), block, block, sibling)

    def do_own(s):
        pass_on(s, (1, 3))

    def do_far(s):
        pass_on(s, (2,))
        loads[s].wait()

    def relay_planes(s, steps):
        for step in steps:
            for by in (1, 3):
                block = here(s, turn(major[s], RING - by), turn(minor[s], RING - step))
                arrived(("g2", s, by, step), block)
                if (step < 2) == (by == 1):
                    send(("g3", s, by, step), block, block, major_peer(s, by))
                send(("pair", s, RING - by, step), block, block, sibling)

    def do_early(s):
        relay_planes(s, (0, 1, 3))

    def do_pass(s):
        relay_planes(s, (2,))

    def do_last(s):
        for step in (0, 3, 1, 2):
            by = 1 if step < 2 else 3
            block = here(s, turn(major[s], 2), turn(minor[s], RING - step))
            arrived(("g3", s, by, step), block)
            send(("pair", s, 2, step), block, block, sibling)

    def places(s, k):
        a = turn(major[s], k)
        return a, turn(x + RING - a, 0)

    def product(s, left, tile):
        if s == 0:
            return jnp.dot(left, wu[:, tile], preferred_element_type=f32)
        return lax.dot_general(
            left, wd[tile, :], (((1,), (1,)), ((), ())), preferred_element_type=f32
        )

    def product_back(s, left, tile):
        if s == 0:
            return jnp.dot(left, wd[:, tile], preferred_element_type=f32)
        return lax.dot_general(
            left, wu[tile, :], (((1,), (1,)), ((), ())), preferred_element_type=f32
        )

    def do_mm(s, k):
        a, m = places(s, k)
        for step in range(RING):
            arrived(("pair", s, k, step), feats.at[s, a, turn(minor[s], RING - step), other])
        left = jnp.concatenate(
            [feats[s, a, turn(m, j)].reshape(32, width) for j in range(RING)], axis=0
        )
        for n in range(hid // BLOCK):
            tile = pl.ds(n * BLOCK, BLOCK)
            value = product(s, left, tile)
            part[s, k, :, :, tile] = value.astype(bf16).reshape(8, 16, BLOCK)
            own_part[s, k, :, :, tile] = value[:32].reshape(2, 16, BLOCK)
        if (s, k) in DIRECT_SUMS:
            for by in (2, 1, 3):
                block = part.at[s, k, pl.ds(2 * by, 2)]
                send(("x1", s, k, by), block, straight.at[s, k, by - 1], row_peer(by))
            return
        send(("x1", s, k, 1), part.at[s, k, pl.ds(3, 2)], relay.at[s, 0, k], row_peer(1))
        send(("x1", s, k, 3), part.at[s, k, pl.ds(5, 2)], relay.at[s, 1, k], row_peer(3))

    def do_comb(s, k):
        for by, side, own, got in ((1, 0, 2, 1), (3, 1, 7, 0)):
            arrived(("x1", s, k, by), relay.at[s, side, k])
            total = part[s, k, own].astype(f32) + relay[s, side, k, got].astype(f32)
            comb_out[s, side, k] = total.astype(bf16)
            send(("x2", s, k, by), comb_out.at[s, side, k], comb_in.at[s, side, k], row_peer(by))

    def do_fin(s, k):
        a, m = places(s, k)
        if (s, k) in DIRECT_SUMS:
            for by in (1, 3, 2):
                arrived(("x1", s, k, by), straight.at[s, k, by - 1])
        else:
            for by, side in ((1, 0), (3, 1)):
                arrived(("x2", s, k, by), comb_in.at[s, side, k])
        for h in (0, 1):
            total = own_part[s, k, h]
            if (s, k) in DIRECT_SUMS:
                for n in range(RING - 1):
                    total = total + straight[s, k, n, h].astype(f32)
            else:
                total = total + relay[s, 1 - h, k, 1 - h].astype(f32) + comb_in[s, h, k].astype(f32)
            if s == 0:
                value, slope = gelu_pair(total)
                hidden[s, a, m, h] = value.astype(bf16)
                slopes[a, h] = slope
            else:
                hidden[s, a, m, h] = (total * slopes[m, h]).astype(bf16)
        block = hidden.at[s, a, m]
        for by in (2, 1, 3) if (s, k) in DIRECT else (1, 3):
            send(("a1", s, k, by), block, block, row_peer(by))

    def do_agf(s, k):
        a, m = places(s, k)
        for by, h in ((1, 0), (3, 1)):
            from_owner = turn(m, RING - by)
            arrived(("a1", s, k, by), hidden.at[s, a, from_owner])
            half = hidden.at[s, a, from_owner, h]
            send(("a2", s, k, by), half, half, row_peer(by))

    def do_om(s, k):
        a, m = places(s, k)
        if (s, k) in DIRECT:
            for by in (1, 3, 2):
                arrived(("a1", s, k, by), hidden.at[s, a, turn(m, RING - by)])
        else:
            for by, h in ((1, 0), (3, 1)):
                arrived(("a2", s, k, by), hidden.at[s, a, turn(m, 2), h])
        places_on = [turn(minor[s], j) for j in range(RING)]
        left = jnp.concatenate([hidden[s, a, m, h] for h in (other, d) for m in places_on], axis=0)
        for n in range(width // BLOCK):
            tile = pl.ds(n * BLOCK, BLOCK)
            value = product_back(s, left, tile)
            pair_out[s, k, :, :, tile] = value[:64].astype(bf16).reshape(RING, 16, BLOCK)
            kept[s, k, :, :, tile] = value[64:].reshape(RING, 16, BLOCK)
        send(("p", s, k), pair_out.at[s, k], pair_in.at[s, k], sibling)

    def do_zs(s, k):
        arrived(("p", s, k), pair_in.at[s, k])
        total = kept[s, k] + pair_in[s, k].astype(f32)
        kept[s, k, 0] = total[0]
        ysend[s, k] = total[1:].astype(bf16)
        for by in (2, 1, 3):
            send(("y", s, k, by), ysend.at[s, k, by - 1], yrecv.at[s, k, by - 1], minor_peer(s, by))

    def do_yg(s, k):
        total = kept[s, k, 0]
        for by in (1, 3, 2):
            arrived(("y", s, k, by), yrecv.at[s, k, by - 1])
            total = total + yrecv[s, k, by - 1].astype(f32)
        if k == 0:
            fown[s] = total
        else:
            fsend[s, k - 1] = total.astype(bf16)
            send(("f", s, k), fsend.at[s, k - 1], frecv.at[s, k - 1], major_peer(s, k))

    def do_yf(s):
        total = fown[s]
        for by in (1, 3, 2):
            arrived(("f", s, by), frecv.at[s, by - 1])
            total = total + frecv[s, by - 1].astype(f32)
        (out_v, gtok_v)[s][...] = total.astype(bf16)

    def do_tt():
        for a in range(RING):
            for n in range(width // BLOCK):
                tile = feats[0, a, :, :, :, pl.ds(n * BLOCK, BLOCK)].reshape(128, BLOCK)
                tok_t[pl.ds(n * BLOCK, BLOCK), pl.ds(a * 128, 128)] = tile.T

    def do_at():
        for a in range(RING):
            for n in range(hid // BLOCK):
                tile = hidden[0, a, :, :, :, pl.ds(n * BLOCK, BLOCK)].reshape(128, BLOCK)
                act_t[pl.ds(n * BLOCK, BLOCK), pl.ds(a * 128, 128)] = tile.T

    def swapped(ref, tile):
        return jnp.concatenate(
            [ref[1, b, a, :, :, tile].reshape(32, BLOCK) for a in range(RING) for b in range(RING)],
            axis=0,
        )

    def do_gdn():
        @pl.loop(0, width // BLOCK)
        def _(fb):
            tile = pl.ds(pl.multiple_of(fb * BLOCK, BLOCK), BLOCK)
            right = swapped(feats, tile)
            for hb in range(hid // BLOCK):
                rows = pl.ds(hb * BLOCK, BLOCK)
                value = jnp.dot(act_t[rows, :], right, preferred_element_type=f32)
                gdown_v[rows, tile] = (value * mask_at(1, hb, fb)).astype(bf16)

    def do_gup(hb):
        tile = pl.ds(hb * BLOCK, BLOCK)
        right = swapped(hidden, tile)

        for half in (0, 1):
            rows = pl.ds(half * (width // 2), width // 2)
            value = jnp.dot(tok_t[rows, :], right, preferred_element_type=f32)
            for n in range(width // 2 // BLOCK):
                fb = half * (width // 2 // BLOCK) + n
                gup_v[pl.ds(fb * BLOCK, BLOCK), tile] = (
                    value[n * BLOCK : (n + 1) * BLOCK] * mask_at(0, hb, fb)
                ).astype(bf16)

    steps = {
        "mask": do_mask, "own": do_own, "far": do_far, "early": do_early, "pass": do_pass, "last": do_last, "mm": do_mm, "comb": do_comb, "fin": do_fin, "agf": do_agf,
        "om": do_om, "zs": do_zs, "yg": do_yg, "yf": do_yf,
        "tt": do_tt, "at": do_at, "gdn": do_gdn, "gup": do_gup,
    }
    for step in SCHEDULE:
        name = step.rstrip("0123")
        steps[name](*[int(v) for v in step[len(name):]])
    for copy in sent:
        copy.wait_send()


def write_out(*refs):
    sources, targets, sems = refs[:4], refs[4:8], refs[8]
    copies = [pltpu.make_async_copy(a, b, sems.at[i]) for i, (a, b) in enumerate(zip(sources, targets))]
    for copy in copies:
        copy.start()
    for copy in copies:
        copy.wait()


def layer(tokens, up_weight, down_weight, grad_out, block_mask):
    rows, width = tokens.shape
    hid = up_weight.shape[1]
    bf16, f32 = jnp.bfloat16, jnp.float32
    V = pltpu.VMEM
    anywhere = pl.BlockSpec(memory_space=pl.ANY)
    block_mask = jnp.transpose(block_mask, (0, 2, 1))
    operands = (tokens, up_weight, down_weight, grad_out, block_mask)
    shapes = ((rows, width), (rows, width), (width, hid), (hid, width))
    results = pl.pallas_call(
        kernel,
        out_shape=[V(shape, bf16) for shape in shapes],
        in_specs=[pl.BlockSpec(memory_space=pltpu.HBM)] * 5,
        out_specs=[pl.BlockSpec(memory_space=V)] * 4,
        scratch_shapes=[
            V((2, 4, 4, 2, 16, width), bf16),
            V((width, hid), bf16),
            V((hid, width), bf16),
            pltpu.SMEM(block_mask.shape, jnp.int32),
            V((2, 4, 8, 16, hid), bf16),
            V((2, 4, 2, 16, hid), f32),
            V((2, 2, 4, 2, 16, hid), bf16),
            V((2, 2, 4, 16, hid), bf16),
            V((2, 2, 4, 16, hid), bf16),
            V((4, 2, 16, hid), f32),
            V((2, 4, 4, 2, 16, hid), bf16),
            V((2, 4, 4, 16, width), bf16),
            V((2, 4, 4, 16, width), bf16),
            V((2, 4, 4, 16, width), f32),
            V((2, 4, 3, 16, width), bf16),
            V((2, 4, 3, 16, width), bf16),
            V((2, 3, 16, width), bf16),
            V((2, 16, width), f32),
            V((2, 3, 16, width), bf16),
            V((2, 4, 3, 2, 16, hid), bf16),
            V((width, 512), bf16),
            V((hid, 512), bf16),
            pltpu.SemaphoreType.DMA((SEMS,)),
            pltpu.SemaphoreType.DMA((SEMS,)),
            pltpu.SemaphoreType.DMA((5,)),
        ],
        compiler_params=pltpu.CompilerParams(
            collective_id=0, has_side_effects=True, vmem_limit_bytes=44 * 1024 * 1024
        ),
        cost_estimate=pl.CostEstimate(
            flops=12 * 512 * width * hid, bytes_accessed=8 * width * hid, transcendentals=0
        ),
    )(*[pltpu.with_memory_space_constraint(v, pltpu.HBM) for v in operands])
    return pl.pallas_call(
        write_out,
        out_shape=[jax.ShapeDtypeStruct(shape, bf16) for shape in shapes],
        in_specs=[anywhere] * 4,
        out_specs=[anywhere] * 4,
        scratch_shapes=[pltpu.SemaphoreType.DMA((4,))],
        compiler_params=pltpu.CompilerParams(vmem_limit_bytes=1024 * 1024),
    )(*results)


def solution(mesh):
    in_specs = (
        P(("depth", "col"), "row"),
        P("row", ("col", "depth")),
        P(("col", "depth"), "row"),
        P(("depth", "col"), "row"),
        P(),
    )
    out_specs = (
        P(("depth", "col"), "row"),
        P(("depth", "col"), "row"),
        P("row", ("col", "depth")),
        P(("col", "depth"), "row"),
    )
    return jax.shard_map(layer, mesh=mesh, in_specs=in_specs, out_specs=out_specs, check_vma=False)
```

```python
import jax
import jax.numpy as jnp
from jax import lax
from jax.experimental import pallas as pl
from jax.experimental.pallas import tpu as pltpu
from jax.sharding import PartitionSpec as P

BLOCK = 256
RING = 4
SEMS = 192
DIRECT_SUMS = ((0, 0), (1, 0))
DIRECT = ((1, 0), (1, 2))
MESH = pl.DeviceIdType.MESH

gelu_scale = 0.7978845608028654
gelu_cubic = 0.044715

SCHEDULE = (
    "mask0", "own0", "own1", "mask1", "far0", "far1", "mm00", "mm10", "early0", "pass0", "early1",
    "mm01", "pass1", "mm03", "mm11", "last0", "mm13", "last1", "mm02", "tt", "fin00", "comb01",
    "comb03", "mm12", "comb02", "comb13", "comb11", "fin01", "fin03", "fin02", "fin11", "comb12",
    "fin13", "agf01", "agf11", "agf03", "agf02", "agf13", "fin12", "agf00", "om01", "om11", "zs01",
    "fin10", "om02", "om03", "zs11", "om13", "zs02", "zs13", "om12", "om00", "zs03", "zs12",
    "om10", "zs00", "zs10", "yg11", "yg02", "yg13", "at", "gup2", "yg01", "yg12", "yg03", "gup0",
    "yg00", "gup1", "gdn", "yg10", "yf1", "yf0",
)


def gelu_pair(pre):
    inner = gelu_scale * (pre + gelu_cubic * pre * pre * pre)
    bend = jnp.tanh(inner)
    value = 0.5 * pre * (1.0 + bend)
    slope = 0.5 * (1.0 + bend) + 0.5 * pre * (1.0 - bend * bend) * gelu_scale * (
        1.0 + 3.0 * gelu_cubic * pre * pre
    )
    return value, slope


def kernel(
    tok_h, up_h, down_h, gout_h, mask_h,
    out_v, gtok_v, gup_v, gdown_v,
    feats, wu, wd, masks, part, own_part, relay, comb_out, comb_in, slopes, hidden,
    pair_out, pair_in, kept, ysend, yrecv, fsend, fown, frecv,
    straight, tok_t, act_t,
    send_sem, recv_sem, local_sem,
):
    f32, bf16 = jnp.float32, jnp.bfloat16
    width = wu.shape[0]
    hid = wu.shape[1]
    x = lax.axis_index("row")
    col = lax.axis_index("col")
    d = lax.axis_index("depth")
    z, y = lax.div(col, RING), lax.rem(col, RING)
    other = 1 - d
    major, minor = (z, y), (y, z)

    def turn(value, by):
        return lax.rem(value + by, RING)

    def major_peer(s, by):
        return {"col": turn(z, by) * RING + y} if s == 0 else {"col": z * RING + turn(y, by)}

    def minor_peer(s, by):
        return major_peer(1 - s, by)

    def row_peer(by):
        return {"row": turn(x, by)}

    sibling = {"depth": other}
    numbers = {}

    def remote(name, src, dst, peer):
        n = numbers.setdefault(name, len(numbers))
        return pltpu.make_async_remote_copy(
            src_ref=src, dst_ref=dst, send_sem=send_sem.at[n], recv_sem=recv_sem.at[n],
            device_id=peer, device_id_type=MESH,
        )

    sent = []

    def send(name, src, dst, peer):
        copy = remote(name, src, dst, peer)
        copy.start()
        sent.append(copy)

    def arrived(name, dst):
        remote(name, dst, dst, sibling).wait_recv()

    sources = (tok_h, gout_h)
    peers = [row_peer(1), row_peer(2), row_peer(3), sibling]
    for by in (1, 2, 3):
        peers += [minor_peer(0, by), minor_peer(1, by)]
    barrier = pltpu.get_barrier_semaphore()
    for peer in peers:
        pl.semaphore_signal(barrier, inc=1, device_id=peer, device_id_type=MESH)
    loads = [
        pltpu.make_async_copy(sources[0], feats.at[0, z, y, d], local_sem.at[0]),
        pltpu.make_async_copy(sources[1], feats.at[1, y, z, d], local_sem.at[1]),
        pltpu.make_async_copy(up_h, wu, local_sem.at[2]),
        pltpu.make_async_copy(mask_h, masks, local_sem.at[4]),
        pltpu.make_async_copy(down_h, wd, local_sem.at[3]),
    ]
    for n in (0, 1, 3):
        loads[n].start()
    pl.semaphore_wait(barrier, len(peers))

    hidden_corner = (col * 2 + d) * (hid // BLOCK)
    feature_corner = x * (width // BLOCK)

    def mask_at(which, hb, fb):
        return masks[which, feature_corner + fb, hidden_corner + hb].astype(f32)

    def here(s, a, m):
        return feats.at[s, a, m, d]

    for s in (0, 1):
        for by in (1, 3, 2):
            send(("g1", s, by), sources[s], here(s, major[s], minor[s]), minor_peer(s, by))
    for s in (0, 1):
        mine = here(s, major[s], minor[s])
        for by in (1, 3):
            send(("g2", s, by, 0), sources[s], mine, major_peer(s, by))
        send(("pair", s, 0, 0), sources[s], mine, sibling)

    loads[2].start()
    loads[4].start()
    loads[3].wait()

    def do_mask(which):
        loads[(2, 4)[which]].wait()
        for fb in range(width // BLOCK):
            for hb in range(hid // BLOCK):
                features, units = pl.ds(fb * BLOCK, BLOCK), pl.ds(hb * BLOCK, BLOCK)
                held, tile = ((wu, (features, units)), (wd, (units, features)))[which]
                held[tile] = held[tile] * mask_at(which, hb, fb).astype(bf16)

    def pass_on(s, steps):
        for step in steps:
            m = turn(minor[s], RING - step)
            block = here(s, major[s], m)
            arrived(("g1", s, step), block)
            for by in (1, 3):
                send(("g2", s, by, step), block, block, major_peer(s, by))
            send(("pair", s, 0, step), block, block, sibling)

    def do_own(s):
        pass_on(s, (1, 3))

    def do_far(s):
        pass_on(s, (2,))
        loads[s].wait()

    def relay_planes(s, steps):
        for step in steps:
            for by in (1, 3):
                block = here(s, turn(major[s], RING - by), turn(minor[s], RING - step))
                arrived(("g2", s, by, step), block)
                if (step < 2) == (by == 1):
                    send(("g3", s, by, step), block, block, major_peer(s, by))
                send(("pair", s, RING - by, step), block, block, sibling)

    def do_early(s):
        relay_planes(s, (0, 1, 3))

    def do_pass(s):
        relay_planes(s, (2,))

    def do_last(s):
        for step in (0, 3, 1, 2):
            by = 1 if step < 2 else 3
            block = here(s, turn(major[s], 2), turn(minor[s], RING - step))
            arrived(("g3", s, by, step), block)
            send(("pair", s, 2, step), block, block, sibling)

    def places(s, k):
        a = turn(major[s], k)
        return a, turn(x + RING - a, 0)

    def product(s, left, tile):
        if s == 0:
            return jnp.dot(left, wu[:, tile], preferred_element_type=f32)
        return lax.dot_general(
            left, wd[tile, :], (((1,), (1,)), ((), ())), preferred_element_type=f32
        )

    def product_back(s, left, tile):
        if s == 0:
            return jnp.dot(left, wd[:, tile], preferred_element_type=f32)
        return lax.dot_general(
            left, wu[tile, :], (((1,), (1,)), ((), ())), preferred_element_type=f32
        )

    def do_mm(s, k):
        a, m = places(s, k)
        for step in range(RING):
            arrived(("pair", s, k, step), feats.at[s, a, turn(minor[s], RING - step), other])
        left = jnp.concatenate(
            [feats[s, a, turn(m, j)].reshape(32, width) for j in range(RING)], axis=0
        )
        for n in range(hid // BLOCK):
            tile = pl.ds(n * BLOCK, BLOCK)
            value = product(s, left, tile)
            part[s, k, :, :, tile] = value.astype(bf16).reshape(8, 16, BLOCK)
            own_part[s, k, :, :, tile] = value[:32].reshape(2, 16, BLOCK)
        if (s, k) in DIRECT_SUMS:
            for by in (2, 1, 3):
                block = part.at[s, k, pl.ds(2 * by, 2)]
                send(("x1", s, k, by), block, straight.at[s, k, by - 1], row_peer(by))
            return
        send(("x1", s, k, 1), part.at[s, k, pl.ds(3, 2)], relay.at[s, 0, k], row_peer(1))
        send(("x1", s, k, 3), part.at[s, k, pl.ds(5, 2)], relay.at[s, 1, k], row_peer(3))

    def do_comb(s, k):
        for by, side, own, got in ((1, 0, 2, 1), (3, 1, 7, 0)):
            arrived(("x1", s, k, by), relay.at[s, side, k])
            total = part[s, k, own].astype(f32) + relay[s, side, k, got].astype(f32)
            comb_out[s, side, k] = total.astype(bf16)
            send(("x2", s, k, by), comb_out.at[s, side, k], comb_in.at[s, side, k], row_peer(by))

    def do_fin(s, k):
        a, m = places(s, k)
        if (s, k) in DIRECT_SUMS:
            for by in (1, 3, 2):
                arrived(("x1", s, k, by), straight.at[s, k, by - 1])
        else:
            for by, side in ((1, 0), (3, 1)):
                arrived(("x2", s, k, by), comb_in.at[s, side, k])
        for h in (0, 1):
            total = own_part[s, k, h]
            if (s, k) in DIRECT_SUMS:
                for n in range(RING - 1):
                    total = total + straight[s, k, n, h].astype(f32)
            else:
                total = total + relay[s, 1 - h, k, 1 - h].astype(f32) + comb_in[s, h, k].astype(f32)
            if s == 0:
                value, slope = gelu_pair(total)
                hidden[s, a, m, h] = value.astype(bf16)
                slopes[a, h] = slope
            else:
                hidden[s, a, m, h] = (total * slopes[m, h]).astype(bf16)
        block = hidden.at[s, a, m]
        for by in (2, 1, 3) if (s, k) in DIRECT else (1, 3):
            send(("a1", s, k, by), block, block, row_peer(by))

    def do_agf(s, k):
        a, m = places(s, k)
        for by, h in ((1, 0), (3, 1)):
            from_owner = turn(m, RING - by)
            arrived(("a1", s, k, by), hidden.at[s, a, from_owner])
            half = hidden.at[s, a, from_owner, h]
            send(("a2", s, k, by), half, half, row_peer(by))

    def do_om(s, k):
        a, m = places(s, k)
        if (s, k) in DIRECT:
            for by in (1, 3, 2):
                arrived(("a1", s, k, by), hidden.at[s, a, turn(m, RING - by)])
        else:
            for by, h in ((1, 0), (3, 1)):
                arrived(("a2", s, k, by), hidden.at[s, a, turn(m, 2), h])
        places_on = [turn(minor[s], j) for j in range(RING)]
        left = jnp.concatenate([hidden[s, a, m, h] for h in (other, d) for m in places_on], axis=0)
        for n in range(width // BLOCK):
            tile = pl.ds(n * BLOCK, BLOCK)
            value = product_back(s, left, tile)
            pair_out[s, k, :, :, tile] = value[:64].astype(bf16).reshape(RING, 16, BLOCK)
            kept[s, k, :, :, tile] = value[64:].reshape(RING, 16, BLOCK)
        send(("p", s, k), pair_out.at[s, k], pair_in.at[s, k], sibling)

    def do_zs(s, k):
        arrived(("p", s, k), pair_in.at[s, k])
        total = kept[s, k] + pair_in[s, k].astype(f32)
        kept[s, k, 0] = total[0]
        ysend[s, k] = total[1:].astype(bf16)
        for by in (2, 1, 3):
            send(("y", s, k, by), ysend.at[s, k, by - 1], yrecv.at[s, k, by - 1], minor_peer(s, by))

    def do_yg(s, k):
        total = kept[s, k, 0]
        for by in (1, 3, 2):
            arrived(("y", s, k, by), yrecv.at[s, k, by - 1])
            total = total + yrecv[s, k, by - 1].astype(f32)
        if k == 0:
            fown[s] = total
        else:
            fsend[s, k - 1] = total.astype(bf16)
            send(("f", s, k), fsend.at[s, k - 1], frecv.at[s, k - 1], major_peer(s, k))

    def do_yf(s):
        total = fown[s]
        for by in (1, 3, 2):
            arrived(("f", s, by), frecv.at[s, by - 1])
            total = total + frecv[s, by - 1].astype(f32)
        (out_v, gtok_v)[s][...] = total.astype(bf16)

    def do_tt():
        for a in range(RING):
            for n in range(width // BLOCK):
                tile = feats[0, a, :, :, :, pl.ds(n * BLOCK, BLOCK)].reshape(128, BLOCK)
                tok_t[pl.ds(n * BLOCK, BLOCK), pl.ds(a * 128, 128)] = tile.T

    def do_at():
        for a in range(RING):
            for n in range(hid // BLOCK):
                tile = hidden[0, a, :, :, :, pl.ds(n * BLOCK, BLOCK)].reshape(128, BLOCK)
                act_t[pl.ds(n * BLOCK, BLOCK), pl.ds(a * 128, 128)] = tile.T

    def swapped(ref, tile):
        return jnp.concatenate(
            [ref[1, b, a, :, :, tile].reshape(32, BLOCK) for a in range(RING) for b in range(RING)],
            axis=0,
        )

    def do_gdn():
        @pl.loop(0, width // BLOCK)
        def _(fb):
            tile = pl.ds(pl.multiple_of(fb * BLOCK, BLOCK), BLOCK)
            right = swapped(feats, tile)
            for hb in range(hid // BLOCK):
                rows = pl.ds(hb * BLOCK, BLOCK)
                value = jnp.dot(act_t[rows, :], right, preferred_element_type=f32)
                gdown_v[rows, tile] = (value * mask_at(1, hb, fb)).astype(bf16)

    def do_gup(hb):
        tile = pl.ds(hb * BLOCK, BLOCK)
        right = swapped(hidden, tile)

        for half in (0, 1):
            rows = pl.ds(half * (width // 2), width // 2)
            value = jnp.dot(tok_t[rows, :], right, preferred_element_type=f32)
            for n in range(width // 2 // BLOCK):
                fb = half * (width // 2 // BLOCK) + n
                gup_v[pl.ds(fb * BLOCK, BLOCK), tile] = (
                    value[n * BLOCK : (n + 1) * BLOCK] * mask_at(0, hb, fb)
                ).astype(bf16)

    steps = {
        "mask": do_mask, "own": do_own, "far": do_far, "early": do_early, "pass": do_pass, "last": do_last, "mm": do_mm, "comb": do_comb, "fin": do_fin, "agf": do_agf,
        "om": do_om, "zs": do_zs, "yg": do_yg, "yf": do_yf,
        "tt": do_tt, "at": do_at, "gdn": do_gdn, "gup": do_gup,
    }
    for step in SCHEDULE:
        name = step.rstrip("0123")
        steps[name](*[int(v) for v in step[len(name):]])
    for copy in sent:
        copy.wait_send()


def write_out(*refs):
    sources, targets, sems = refs[:4], refs[4:8], refs[8]
    copies = [pltpu.make_async_copy(a, b, sems.at[i]) for i, (a, b) in enumerate(zip(sources, targets))]
    for copy in copies:
        copy.start()
    for copy in copies:
        copy.wait()


def layer(tokens, up_weight, down_weight, grad_out, block_mask):
    rows, width = tokens.shape
    hid = up_weight.shape[1]
    bf16, f32 = jnp.bfloat16, jnp.float32
    V = pltpu.VMEM
    anywhere = pl.BlockSpec(memory_space=pl.ANY)
    block_mask = jnp.transpose(block_mask, (0, 2, 1))
    operands = (tokens, up_weight, down_weight, grad_out, block_mask)
    shapes = ((rows, width), (rows, width), (width, hid), (hid, width))
    results = pl.pallas_call(
        kernel,
        out_shape=[V(shape, bf16) for shape in shapes],
        in_specs=[pl.BlockSpec(memory_space=pltpu.HBM)] * 5,
        out_specs=[pl.BlockSpec(memory_space=V)] * 4,
        scratch_shapes=[
            V((2, 4, 4, 2, 16, width), bf16),
            V((width, hid), bf16),
            V((hid, width), bf16),
            pltpu.SMEM(block_mask.shape, jnp.int32),
            V((2, 4, 8, 16, hid), bf16),
            V((2, 4, 2, 16, hid), f32),
            V((2, 2, 4, 2, 16, hid), bf16),
            V((2, 2, 4, 16, hid), bf16),
            V((2, 2, 4, 16, hid), bf16),
            V((4, 2, 16, hid), f32),
            V((2, 4, 4, 2, 16, hid), bf16),
            V((2, 4, 4, 16, width), bf16),
            V((2, 4, 4, 16, width), bf16),
            V((2, 4, 4, 16, width), f32),
            V((2, 4, 3, 16, width), bf16),
            V((2, 4, 3, 16, width), bf16),
            V((2, 3, 16, width), bf16),
            V((2, 16, width), f32),
            V((2, 3, 16, width), bf16),
            V((2, 4, 3, 2, 16, hid), bf16),
            V((width, 512), bf16),
            V((hid, 512), bf16),
            pltpu.SemaphoreType.DMA((SEMS,)),
            pltpu.SemaphoreType.DMA((SEMS,)),
            pltpu.SemaphoreType.DMA((5,)),
        ],
        compiler_params=pltpu.CompilerParams(
            collective_id=0, has_side_effects=True, vmem_limit_bytes=44 * 1024 * 1024
        ),
        cost_estimate=pl.CostEstimate(
            flops=12 * 512 * width * hid, bytes_accessed=8 * width * hid, transcendentals=0
        ),
    )(*[pltpu.with_memory_space_constraint(v, pltpu.HBM) for v in operands])
    return pl.pallas_call(
        write_out,
        out_shape=[jax.ShapeDtypeStruct(shape, bf16) for shape in shapes],
        in_specs=[anywhere] * 4,
        out_specs=[anywhere] * 4,
        scratch_shapes=[pltpu.SemaphoreType.DMA((4,))],
        compiler_params=pltpu.CompilerParams(vmem_limit_bytes=1024 * 1024),
    )(*results)


def solution(mesh):
    in_specs = (
        P(("depth", "col"), "row"),
        P("row", ("col", "depth")),
        P(("col", "depth"), "row"),
        P(("depth", "col"), "row"),
        P(),
    )
    out_specs = (
        P(("depth", "col"), "row"),
        P(("depth", "col"), "row"),
        P("row", ("col", "depth")),
        P(("col", "depth"), "row"),
    )
    return jax.shard_map(layer, mesh=mesh, in_specs=in_specs, out_specs=out_specs, check_vma=False)
```
